512 devices in a mesh: group: 4 (over z_lo), dp: 32 (over y, x, core), mp: 4 (over z_hi).
Axes of the slice: x: 4, y: 4, z: 16 (z_hi: 4, z_lo: 4; z = z_hi * 4 + z_lo), core: 2. Of those that a mesh axis runs over, the one named last changes fastest.
Arguments:
- dino_context: bfloat16 [256, 128, 1536], P('group', 'dp', 'mp'), may hold values from -6 to 6
- dino_stream: bfloat16 [256, 128, 1536], P('group', 'dp', 'mp'), may hold values from -6 to 6
- dino_out_proj: bfloat16 [1536, 1536], P('dp', 'mp'), may hold values from -0.15625 to 0.15625
- sam_context: bfloat16 [256, 128, 1280], P('group', 'dp', 'mp'), may hold values from -6 to 6
- sam_stream: bfloat16 [256, 128, 1280], P('group', 'dp', 'mp'), may hold values from -6 to 6
- sam_out_proj: bfloat16 [1280, 1280], P('dp', 'mp'), may hold values from -0.15625 to 0.15625
- owners: int32 [4, 64], P('group'), may hold values from 0 to 63, each once within a row
- valid_rows: int32 [256], P(('group', 'dp')), may hold values from 32 to 128, as said below
- student_stream: bfloat16 [256, 128, 1280], P(('group', 'dp'), None, 'mp'), may hold values from -6 to 6
- norm_gain: float32 [1280], P('mp'), may hold values from 0.1 to 1.9
- adapt_dino: bfloat16 [1280, 1536], P(None, 'mp'), may hold values from -0.15625 to 0.15625
- adapt_dino_bias: float32 [1536], P('mp'), may hold values from -4 to 4
- adapt_sam: bfloat16 [1280, 1280], P(None, 'mp'), may hold values from -0.15625 to 0.15625
- adapt_sam_bias: float32 [1280], P('mp'), may hold values from -4 to 4
Outputs:
- stream_grad: bfloat16 [256, 128, 1280], P(('group', 'dp'), None, 'mp')
- dino_head_grad: bfloat16 [1280, 1536], P(('group', 'dp'), 'mp')
- dino_bias_grad: float32 [1536], P('mp')
- sam_head_grad: bfloat16 [1280, 1280], P(('group', 'dp'), 'mp')
- sam_bias_grad: float32 [1280], P('mp')
- gain_grad: float32 [1280], P('mp')
The draws below stay inside these ranges and needn't reach their ends.
Inputs may be any that keep to these rules, and one draw needn't show every extreme that they name: `valid_rows`: rows of a slot at or past its count are padding; some slot has all 128 rows and some has 32. `owners`: each row is a permutation of the slots of its slab.
All inputs are finite; a program needn't handle non-finite values.
Results may differ from the reference program's by a relative error of at most 0.017.
Values may be sent and summed in bfloat16 or wider, within the bound.
No kernel may reach another device: no remote copies, remote signals or barrier semaphores. Data moves between devices by JAX's collectives and lax.ppermute only.
A program may use at most 64 MiB of HBM per device.

```python
import jax
import jax.numpy as jnp
from jax import lax

DT = 1536
DS = 1280
WINDOW_ROWS = 128
SLOTS_DEV = 2
IMAGES = 256
N_GROUP = 4
N_DP = 32


def draw_valid_rows(key, part):
    key = jax.random.fold_in(key, 7)
    counts = jax.random.randint(key, (IMAGES,), WINDOW_ROWS // 4, WINDOW_ROWS + 1)
    counts = counts.at[0].set(WINDOW_ROWS)
    counts = counts.at[1].set(WINDOW_ROWS // 4)
    return counts.astype(jnp.int32)


def block_scale(key, extent, shards, low, largest):
    factor_of, own = 1.0, jax.random.fold_in(key, 6)
    for position, shards_of in shards:
        heights = jnp.exp(jax.random.uniform(jax.random.fold_in(own, position), (shards_of,), jnp.float32, low / len(shards), largest / len(shards)))
        factor_of = factor_of * jnp.repeat(heights, extent[position] // shards_of).reshape([-1 if axis == position else 1 for axis in range(len(extent))])
    return factor_of


def scatter_about(stream_key, dims, deviation, most, split=(), kind=jnp.bfloat16):
    array = jax.random.normal(stream_key, dims, jnp.float32) * deviation
    if len(split) > 0:
        array = block_scale(stream_key, dims, split, -0.22, 0.18) * array
    return jnp.clip(array, min=-most, max=most).astype(kind)


def setup_inputs(seed: int = 0) -> dict:
    arg_keys = jax.random.split(jax.random.key(seed), 15)
    dino_context = scatter_about(arg_keys[0], (IMAGES, WINDOW_ROWS, DT), 1.0, 6.0, ((0, 4), (1, 32), (2, 4)))
    dino_stream = scatter_about(arg_keys[1], (IMAGES, WINDOW_ROWS, DT), 1.0, 6.0, ((0, 4), (1, 32), (2, 4)))
    dino_out_proj = scatter_about(arg_keys[2], (DT, DT), DT ** -0.5, 0.15625, ((0, 32), (1, 4)))
    sam_context = scatter_about(arg_keys[3], (IMAGES, WINDOW_ROWS, DS), 1.0, 6.0, ((0, 4), (1, 32), (2, 4)))
    sam_stream = scatter_about(arg_keys[4], (IMAGES, WINDOW_ROWS, DS), 1.0, 6.0, ((0, 4), (1, 32), (2, 4)))
    sam_out_proj = scatter_about(arg_keys[5], (DS, DS), DS ** -0.5, 0.15625, ((0, 32), (1, 4)))
    owners = jax.vmap(lambda own: jax.random.permutation(own, N_DP * SLOTS_DEV))(jax.random.split(arg_keys[6], N_GROUP)).reshape((N_GROUP, N_DP * SLOTS_DEV)).astype(jnp.int32)
    valid_rows = draw_valid_rows(jax.random.fold_in(arg_keys[14], 71), 0)
    student_stream = scatter_about(arg_keys[8], (IMAGES, WINDOW_ROWS, DS), 1.0, 6.0, ((0, 128), (2, 4)))
    norm_gain = jnp.clip(1.0 + 0.18 * jax.random.normal(arg_keys[9], (DS,), jnp.float32), 0.1, 1.9)
    adapt_dino = scatter_about(arg_keys[10], (DS, DT), DS ** -0.5, 0.15625, ((1, 4),))
    adapt_dino_bias = scatter_about(arg_keys[11], (DT,), 0.7, 4.0, ((0, 4),), jnp.float32)
    adapt_sam = scatter_about(arg_keys[12], (DS, DS), DS ** -0.5, 0.15625, ((1, 4),))
    adapt_sam_bias = scatter_about(arg_keys[13], (DS,), 0.7, 4.0, ((0, 4),), jnp.float32)
    return dict(dino_context=dino_context, dino_stream=dino_stream, dino_out_proj=dino_out_proj, sam_context=sam_context, sam_stream=sam_stream, sam_out_proj=sam_out_proj, owners=owners, valid_rows=valid_rows, student_stream=student_stream, norm_gain=norm_gain, adapt_dino=adapt_dino, adapt_dino_bias=adapt_dino_bias, adapt_sam=adapt_sam, adapt_sam_bias=adapt_sam_bias)


eps = 1e-06
loss_weight = 1024.0

def teacher(context, stream, proj):
    flat = context.reshape(-1, context.shape[-1])
    mixed = jnp.dot(flat, proj, preferred_element_type=jnp.float32)
    total = stream.reshape(flat.shape[0], -1).astype(jnp.float32) + mixed
    return total.astype(jnp.bfloat16).reshape(stream.shape)

def head_grad(out, target, live):
    inner = lax.optimization_barrier(jnp.sum(out * target, axis=1, keepdims=True))
    square = lax.optimization_barrier(jnp.sum(out * out, axis=1, keepdims=True))
    tsquare = lax.optimization_barrier(jnp.sum(target * target, axis=1, keepdims=True))
    inverse = lax.rsqrt(square + eps) * lax.rsqrt(tsquare + eps)
    cosine = inner * inverse
    return -loss_weight * live * (target * inverse - cosine * out / (square + eps))

def reference(dino_context, dino_stream, dino_out_proj, sam_context, sam_stream, sam_out_proj, owners, valid_rows, student_stream, norm_gain, adapt_dino, adapt_dino_bias, adapt_sam, adapt_sam_bias):
    dino_feat = teacher(dino_context, dino_stream, dino_out_proj)
    sam_feat = teacher(sam_context, sam_stream, sam_out_proj)
    groups, width = owners.shape
    inverse = jnp.argsort(owners, axis=1).astype(jnp.int32)
    order = (jnp.arange(groups, dtype=jnp.int32)[:, None] * width + inverse).reshape(-1)
    dino_target = dino_feat[order].reshape(-1, dino_feat.shape[-1]).astype(jnp.float32)
    sam_target = sam_feat[order].reshape(-1, sam_feat.shape[-1]).astype(jnp.float32)
    images, rows, feats = student_stream.shape
    live = (jnp.arange(rows, dtype=jnp.int32)[None, :] < valid_rows[:, None]).astype(jnp.float32).reshape(-1, 1)
    values = student_stream.reshape(-1, feats).astype(jnp.float32)
    center = lax.optimization_barrier(jnp.sum(values, axis=1, keepdims=True)) / feats
    spread = lax.optimization_barrier(jnp.sum(values * values, axis=1, keepdims=True)) / feats - center * center
    scale = lax.rsqrt(spread + eps)
    standard = (values - center) * scale
    normed = (standard * norm_gain[None, :]).astype(jnp.bfloat16)
    dino_out = jnp.dot(normed, adapt_dino, preferred_element_type=jnp.float32) + adapt_dino_bias[None, :]
    sam_out = jnp.dot(normed, adapt_sam, preferred_element_type=jnp.float32) + adapt_sam_bias[None, :]
    dino_grad = head_grad(dino_out, dino_target, live)
    sam_grad = head_grad(sam_out, sam_target, live)
    dino_back = dino_grad.astype(jnp.bfloat16)
    sam_back = sam_grad.astype(jnp.bfloat16)
    normed_grad = jnp.dot(dino_back, adapt_dino.T, preferred_element_type=jnp.float32) + jnp.dot(sam_back, adapt_sam.T, preferred_element_type=jnp.float32)
    scaled = normed_grad * norm_gain[None, :]
    first_sum = lax.optimization_barrier(jnp.sum(scaled, axis=1, keepdims=True)) / feats
    second_sum = lax.optimization_barrier(jnp.sum(scaled * standard, axis=1, keepdims=True)) / feats
    stream_grad = ((scaled - first_sum - standard * second_sum) * scale).astype(jnp.bfloat16).reshape(images, rows, feats)
    factor = lax.rsqrt(jnp.sum(live))
    dino_head_grad = (factor * jnp.dot(normed.T, dino_back, preferred_element_type=jnp.float32)).astype(jnp.bfloat16)
    sam_head_grad = (factor * jnp.dot(normed.T, sam_back, preferred_element_type=jnp.float32)).astype(jnp.bfloat16)
    dino_bias_grad = factor * lax.optimization_barrier(jnp.sum(dino_grad, axis=0))
    sam_bias_grad = factor * lax.optimization_barrier(jnp.sum(sam_grad, axis=0))
    gain_grad = factor * lax.optimization_barrier(jnp.sum(normed_grad * standard, axis=0))
    return (stream_grad, dino_head_grad, dino_bias_grad, sam_head_grad, sam_bias_grad, gain_grad)
```

```python
import jax
import jax.numpy as jnp
from jax import lax
from jax.sharding import Mesh
from jax.sharding import PartitionSpec as P

eps = 1e-06
loss_weight = 1024.0
f32 = jnp.float32
bf16 = jnp.bfloat16

EXTENT = {"g": 4, "y": 4, "x": 4, "c": 2, "m": 4}
DP = ("y", "x", "c")


def shift(array, axis, by):
    extent = EXTENT[axis]
    return lax.ppermute(array, axis, [(i, (i + by) % extent) for i in range(extent)])


def dot(a, b):
    return jnp.dot(a, b, preferred_element_type=f32)


def dot_last(a, b):
    return lax.dot_general(a, b, (((1,), (1,)), ((), ())), preferred_element_type=f32)


def dot_rows(a, b):
    return lax.dot_general(a, b, (((0,), (0,)), ((), ())), preferred_element_type=f32)


def ring_m(block):
    before = shift(block, "m", 1)
    after = shift(block, "m", -1)
    half = block.shape[0] // 2
    far = jnp.concatenate([shift(before[:half], "m", 1), shift(after[half:], "m", -1)], axis=0)
    return [block, after, far, before]


def gather_axis(block, axis):
    extent = EXTENT[axis]
    here = lax.axis_index(axis)
    whole = jnp.zeros((extent,) + block.shape, block.dtype)
    whole = lax.dynamic_update_index_in_dim(whole, block, here, 0)
    for by in range(1, extent):
        whole = lax.dynamic_update_index_in_dim(
            whole, shift(block, axis, by), (here - by) % extent, 0
        )
    return whole


def sum_axis(array, axis):
    total = array
    for by in range(1, EXTENT[axis]):
        total = total + shift(array, axis, by)
    return total


def one_hot(picked, width):
    return (lax.broadcasted_iota(jnp.int32, (picked.shape[0], width), 1) == picked[:, None]).astype(
        bf16
    )


def head_grad(out, target, inner, square, tsquare, live):
    inverse = lax.rsqrt(square + eps) * lax.rsqrt(tsquare + eps)
    cosine = inner * inverse
    return -loss_weight * live * (target * inverse - cosine * out / (square + eps))


def local(
    dino_context,
    dino_stream,
    dino_out_proj,
    sam_context,
    sam_stream,
    sam_out_proj,
    owners,
    valid_rows,
    student_stream,
    norm_gain,
    adapt_dino,
    adapt_dino_bias,
    adapt_sam,
    adapt_sam_bias,
):
    m = lax.axis_index("m")
    c = lax.axis_index("c")
    slots, per_peer, wd = dino_context.shape
    ws = sam_context.shape[2]
    rows = slots * per_peer
    own_slots, window, wf = student_stream.shape
    feats = wf * EXTENT["m"]
    peers = slots // own_slots

    student = ring_m(student_stream.reshape(rows, wf))
    dino_blocks = ring_m(dino_context.reshape(rows, wd))
    sam_blocks = ring_m(sam_context.reshape(rows, ws))
    gains = [norm_gain] + [shift(norm_gain, "m", -by) for by in range(1, EXTENT["m"])]

    kd, ks = dino_out_proj.shape[0], sam_out_proj.shape[0]
    packed = jnp.concatenate(
        [dino_out_proj, jnp.pad(sam_out_proj, ((0, 0), (0, wd - ws)))], axis=0
    )
    plane = gather_axis(gather_axis(packed, "x"), "y")
    other = shift(plane, "c", 1)
    proj = jnp.stack(
        [jnp.where(c == 0, plane, other), jnp.where(c == 0, other, plane)], axis=2
    )
    dino_proj = proj[:, :, :, :kd, :].reshape(EXTENT["m"], -1, wd)
    sam_proj = proj[:, :, :, kd:, :ws].reshape(EXTENT["m"], -1, ws)

    dino_mixed = sum(
        dot(dino_blocks[by], lax.dynamic_index_in_dim(dino_proj, (m + by) % 4, 0, False))
        for by in range(4)
    )
    sam_mixed = sum(
        dot(sam_blocks[by], lax.dynamic_index_in_dim(sam_proj, (m + by) % 4, 0, False))
        for by in range(4)
    )
    dino_feat = (dino_stream.reshape(rows, wd).astype(f32) + dino_mixed).astype(bf16)
    sam_feat = (sam_stream.reshape(rows, ws).astype(f32) + sam_mixed).astype(bf16)
    feat = jnp.concatenate([dino_feat, sam_feat], axis=1)
    order = jnp.argsort(owners[0]).astype(jnp.int32)
    wanted = (order[:, None] * per_peer + jnp.arange(per_peer, dtype=jnp.int32)[None, :]).reshape(-1)
    sent = dot(one_hot(wanted, rows), feat).astype(bf16)
    arrived = lax.all_to_all(sent, DP, split_axis=0, concat_axis=0, tiled=True)
    place = jnp.arange(rows, dtype=jnp.int32)
    slot, row = place // window, place % window
    source = (row // per_peer) * (own_slots * per_peer) + slot * per_peer + row % per_peer
    target = dot(one_hot(source, rows), arrived)
    dino_target, sam_target = target[:, :wd], target[:, wd:]

    live = (
        (jnp.arange(window, dtype=jnp.int32)[None, :] < valid_rows[:, None])
        .astype(f32)
        .reshape(rows, 1)
    )
    values = [block.astype(f32) for block in student]
    total = sum(jnp.sum(block, axis=1, keepdims=True) for block in values)
    squares = sum(jnp.sum(block * block, axis=1, keepdims=True) for block in values)
    center = total / feats
    spread = squares / feats - center * center
    scale = lax.rsqrt(spread + eps)
    values = jnp.concatenate(values, axis=1)
    gain = jnp.concatenate(gains)[None, :]
    standard = (values - center) * scale
    normed = (standard * gain).astype(bf16)
    adapt = jnp.roll(
        jnp.concatenate([adapt_dino, adapt_sam], axis=1).reshape(EXTENT["m"], wf, wd + ws), -m, axis=0
    ).reshape(feats, wd + ws)
    out = dot(normed, adapt) + jnp.concatenate([adapt_dino_bias, adapt_sam_bias])[None, :]
    dino_out, sam_out = out[:, :wd], out[:, wd:]
    spot = jnp.arange(feats, dtype=jnp.int32)
    each = feats // (EXTENT["g"] * peers)
    i, rest = spot % each, spot // each
    g_of, rest = rest % 4, rest // 4
    x_of, rest = rest % 4, rest // 4
    y_of, c_of = rest % 4, rest // 4
    feature = (((g_of * 4 + y_of) * 4 + x_of) * 2 + c_of) * each + i
    where_now = ((feature // wf - m) % 4) * wf + feature % wf
    dealt = dot_last(normed, one_hot(where_now, feats)).astype(bf16)

    stats = lax.psum(
        jnp.stack(
            [
                jnp.sum(dino_out * dino_target, axis=1),
                jnp.sum(dino_out * dino_out, axis=1),
                jnp.sum(dino_target * dino_target, axis=1),
                jnp.sum(sam_out * sam_target, axis=1),
                jnp.sum(sam_out * sam_out, axis=1),
                jnp.sum(sam_target * sam_target, axis=1),
            ]
        ),
        "m",
    )[:, :, None]
    dino_grad = head_grad(dino_out, dino_target, stats[0], stats[1], stats[2], live)
    sam_grad = head_grad(sam_out, sam_target, stats[3], stats[4], stats[5], live)
    grad = jnp.concatenate([dino_grad, sam_grad], axis=1)
    back = grad.astype(bf16)

    weight = dot_rows(dealt, back)
    half = feats // 2
    mine = lax.dynamic_slice_in_dim(weight, c * half, half, 0)
    theirs = lax.dynamic_slice_in_dim(weight, (1 - c) * half, half, 0).astype(bf16)
    chip = (mine + shift(theirs, "c", 1).astype(f32)).astype(bf16)
    dealt_xy = lax.all_to_all(chip, ("y", "x"), split_axis=0, concat_axis=0, tiled=True)
    slab = jnp.sum(dealt_xy.reshape(16, -1, wd + ws).astype(f32), axis=0).astype(bf16)
    share = sum(
        piece.astype(f32)
        for piece in [lax.dynamic_slice_in_dim(slab, lax.axis_index("g") * each, each, 0)]
        + [
            shift(
                lax.dynamic_slice_in_dim(slab, ((lax.axis_index("g") + by) % 4) * each, each, 0),
                "g",
                by,
            )
            for by in range(1, 4)
        ]
    )

    partial = dot_last(back, adapt)
    scaled_part = partial * gain
    first_part = jnp.sum(scaled_part, axis=1)
    second_part = jnp.sum(scaled_part * standard, axis=1)
    gain_part = jnp.sum(partial * standard, axis=0)
    partial_low = partial.astype(bf16)
    normed_grad = partial[:, :wf]
    small = jnp.concatenate([first_part, second_part, gain_part[:wf]])
    for by in range(1, EXTENT["m"]):
        block = slice(by * wf, (by + 1) * wf)
        normed_grad = normed_grad + shift(partial_low[:, block], "m", by).astype(f32)
        small = small + shift(
            jnp.concatenate([first_part, second_part, gain_part[block]]), "m", by
        )
    first_sum = small[:rows, None] / feats
    second_sum = small[rows : 2 * rows, None] / feats
    own_standard = standard[:, :wf]
    scaled = normed_grad * norm_gain[None, :]
    stream_grad = ((scaled - first_sum - own_standard * second_sum) * scale).astype(bf16)

    vector = jnp.concatenate([jnp.sum(grad, axis=0), small[2 * rows :], jnp.sum(live).reshape(1)])
    for axis in ("c", "x", "y", "g"):
        vector = sum_axis(vector, axis)
    factor = lax.rsqrt(vector[-1])
    vector = factor * vector[:-1]
    share = (factor * share).astype(bf16)
    return (
        stream_grad.reshape(own_slots, window, wf),
        share[:, :wd],
        vector[:wd],
        share[:, wd:],
        vector[wd : wd + ws],
        vector[wd + ws :],
    )


def solution(mesh):
    parts = Mesh(
        mesh.devices.reshape(tuple(EXTENT[axis] for axis in ("g", "y", "x", "c", "m"))),
        ("g", "y", "x", "c", "m"),
    )
    every = ("g",) + DP
    placed = (
        P("g", DP, "m"),
        P("g", DP, "m"),
        P(DP, "m"),
        P("g", DP, "m"),
        P("g", DP, "m"),
        P(DP, "m"),
        P("g", None),
        P(every),
        P(every, None, "m"),
        P("m"),
        P(None, "m"),
        P("m"),
        P(None, "m"),
        P("m"),
    )
    return jax.shard_map(
        local,
        mesh=parts,
        in_specs=placed,
        out_specs=(
            P(every, None, "m"),
            P(every, "m"),
            P("m"),
            P(every, "m"),
            P("m"),
            P("m"),
        ),
        check_vma=False,
    )
```

```python
import jax
import jax.numpy as jnp
from jax import lax
from jax.sharding import Mesh
from jax.sharding import PartitionSpec as P

eps = 1e-06
loss_weight = 1024.0
f32 = jnp.float32
bf16 = jnp.bfloat16

EXTENT = {"g": 4, "y": 4, "x": 4, "c": 2, "m": 4}
DP = ("y", "x", "c")


def swap(array):
    return lax.ppermute(array, "c", [(0, 1), (1, 0)])


def exchange(array, axis):
    return lax.all_to_all(array, axis, split_axis=0, concat_axis=0, tiled=True)


def dot(a, b):
    return jnp.dot(a, b, preferred_element_type=f32)


def dot_last(a, b):
    return lax.dot_general(a, b, (((1,), (1,)), ((), ())), preferred_element_type=f32)


def dot_rows(a, b):
    return lax.dot_general(a, b, (((0,), (0,)), ((), ())), preferred_element_type=f32)


def one_hot(picked, width):
    return (lax.broadcasted_iota(jnp.int32, (picked.shape[0], width), 1) == picked[:, None]).astype(
        bf16
    )


def split(array, count):
    terms = []
    for _ in range(count):
        term = lax.reduce_precision(array, 8, 7)
        terms.append(term.astype(bf16))
        array = array - term
    return terms


def to_rows(vector, width):
    terms = jnp.concatenate(split(vector, 2))
    rows = -(-terms.shape[0] // (8 * width)) * 8
    return jnp.pad(terms, (0, rows * width - terms.shape[0])).reshape(rows, width)


def from_rows(rows, length):
    terms = rows.astype(f32).reshape(*rows.shape[:-2], -1)
    return terms[..., :length] + terms[..., length : 2 * length]


def head_grad(out, target, inner, square, tsquare, live):
    inverse = lax.rsqrt(square + eps) * lax.rsqrt(tsquare + eps)
    cosine = inner * inverse
    return -loss_weight * live * (target * inverse - cosine * out / (square + eps))


def local(
    dino_context,
    dino_stream,
    dino_out_proj,
    sam_context,
    sam_stream,
    sam_out_proj,
    owners,
    valid_rows,
    student_stream,
    norm_gain,
    adapt_dino,
    adapt_dino_bias,
    adapt_sam,
    adapt_sam_bias,
):
    m, c = lax.axis_index("m"), lax.axis_index("c")
    slots, per_peer, wd = dino_context.shape
    ws = sam_context.shape[2]
    rows = slots * per_peer
    own_slots, window, wf = student_stream.shape
    wt = wd + ws
    feats = wf * EXTENT["m"]
    peers = slots // own_slots
    kd, ks = dino_out_proj.shape[0], sam_out_proj.shape[0]

    gain_terms = jnp.pad(jnp.stack(split(norm_gain, 3)), ((0, 5), (0, ws)))
    sam_student = jnp.concatenate(
        [sam_context.reshape(rows, ws), student_stream.reshape(rows, wf)], axis=1
    )
    sam_student = lax.all_gather(
        jnp.concatenate([sam_student, gain_terms], axis=0), "m", axis=0, tiled=False
    )
    dino_full = lax.all_gather(dino_context.reshape(rows, wd), "m", axis=1, tiled=True)
    packed = jnp.concatenate(
        [dino_out_proj, jnp.pad(sam_out_proj, ((0, 0), (0, wd - ws)))], axis=0
    )
    proj = exchange(jnp.tile(packed, (peers, 1)), DP).reshape(peers, kd + ks, wd)
    dino_proj = proj[:, :kd].reshape(peers * kd, wd)
    sam_proj = proj[:, kd:, :ws].reshape(peers * ks, ws)

    dino_mixed = dot(dino_full, dino_proj)
    sam_full = jnp.concatenate([sam_student[j, :rows, :ws] for j in range(4)], axis=1)
    sam_mixed = dot(sam_full, sam_proj)
    dino_feat = (dino_stream.reshape(rows, wd).astype(f32) + dino_mixed).astype(bf16)
    sam_feat = (sam_stream.reshape(rows, ws).astype(f32) + sam_mixed).astype(bf16)
    feat = jnp.concatenate([dino_feat, sam_feat], axis=1)
    image_row = jnp.arange(per_peer, dtype=jnp.int32)[None, :]
    goes_to = (owners[0][:, None] * per_peer + image_row).reshape(-1)
    sent = dot_rows(one_hot(goes_to, rows), feat).astype(bf16)
    arrived = exchange(sent, DP)
    place = jnp.arange(rows, dtype=jnp.int32)
    slot, row = place // window, place % window
    source = (row // per_peer) * (own_slots * per_peer) + slot * per_peer + row % per_peer
    target = dot(one_hot(source, rows), arrived)
    dino_target, sam_target = target[:, :wd], target[:, wd:]

    live = (
        (jnp.arange(window, dtype=jnp.int32)[None, :] < valid_rows[:, None])
        .astype(f32)
        .reshape(rows, 1)
    )
    values = jnp.concatenate([sam_student[j, :rows, ws:] for j in range(4)], axis=1).astype(f32)
    terms = sam_student[:, rows : rows + 3, :wf].astype(f32)
    gain = (terms[:, 0] + (terms[:, 1] + terms[:, 2])).reshape(1, feats)
    center = jnp.sum(values, axis=1, keepdims=True) / feats
    spread = jnp.sum(values * values, axis=1, keepdims=True) / feats - center * center
    scale = lax.rsqrt(spread + eps)
    standard = (values - center) * scale
    normed = (standard * gain).astype(bf16)
    adapt = jnp.concatenate([adapt_dino, adapt_sam], axis=1)
    out = dot(normed, adapt) + jnp.concatenate([adapt_dino_bias, adapt_sam_bias])[None, :]
    dino_out, sam_out = out[:, :wd], out[:, wd:]
    each = feats // (EXTENT["g"] * peers)
    spot = jnp.arange(feats, dtype=jnp.int32)
    i, rest = spot % each, spot // each
    g_of, rest = rest % 4, rest // 4
    x_of, rest = rest % 4, rest // 4
    y_of, c_of = rest % 4, (rest // 4 + c) % 2
    feature = (((g_of * 4 + y_of) * 4 + x_of) * 2 + c_of) * each + i
    dealt = dot_last(normed, one_hot(feature, feats)).astype(bf16)

    stats = lax.psum(
        jnp.stack(
            [
                jnp.sum(dino_out * dino_target, axis=1),
                jnp.sum(dino_out * dino_out, axis=1),
                jnp.sum(dino_target * dino_target, axis=1),
                jnp.sum(sam_out * sam_target, axis=1),
                jnp.sum(sam_out * sam_out, axis=1),
                jnp.sum(sam_target * sam_target, axis=1),
            ]
        ),
        "m",
    )[:, :, None]
    dino_grad = head_grad(dino_out, dino_target, stats[0], stats[1], stats[2], live)
    sam_grad = head_grad(sam_out, sam_target, stats[3], stats[4], stats[5], live)
    grad = jnp.concatenate([dino_grad, sam_grad], axis=1)
    back = grad.astype(bf16)

    partial = dot_last(adapt, back)
    low = lax.psum_scatter(partial.astype(bf16), "m", scatter_dimension=0, tiled=True)
    scaled_part = partial * gain.T
    row_sums = jnp.stack(
        [jnp.sum(scaled_part, axis=0), jnp.sum(scaled_part * standard.T, axis=0)]
    )
    gain_part = jnp.sum(partial * standard.T, axis=1)

    half = feats // 2
    length = wt + feats + 1
    vector = jnp.concatenate([jnp.sum(grad, axis=0), gain_part, jnp.sum(live).reshape(1)])
    mine = dot_rows(dealt[:, :half], back)
    theirs = dot_rows(dealt[:, half:], back).astype(bf16)
    received = swap(jnp.concatenate([theirs, to_rows(vector, wt)], axis=0))
    chip = (mine + received[:half].astype(f32)).astype(bf16)
    vector = vector + from_rows(received[half:], length)
    beside = to_rows(vector, wt)
    chip = jnp.concatenate(
        [chip.reshape(16, -1, wt), jnp.broadcast_to(beside[None], (16,) + beside.shape)], axis=1
    )
    chip, row_sums = lax.optimization_barrier((chip, row_sums))
    slab = exchange(chip.reshape(-1, wt), ("y", "x")).reshape(chip.shape)
    row_sums = lax.psum(row_sums, "m")
    strip = 4 * each
    weight = jnp.sum(slab[:, :strip].astype(f32), axis=0).astype(bf16)
    vector = jnp.sum(from_rows(slab[:, strip:], length), axis=0)
    beside = to_rows(vector, wt)
    deal = jnp.concatenate(
        [weight.reshape(4, each, wt), jnp.broadcast_to(beside[None], (4,) + beside.shape)], axis=1
    )
    share = exchange(deal.reshape(-1, wt), "g").reshape(deal.shape)
    weight = jnp.sum(share[:, :each].astype(f32), axis=0)
    vector = jnp.sum(from_rows(share[:, each:], length), axis=0)
    factor = lax.rsqrt(vector[-1])
    weight = (factor * weight).astype(bf16)
    gain_grad = factor * lax.psum_scatter(vector[wt:-1], "m", scatter_dimension=0, tiled=True)

    own = student_stream.reshape(rows, wf).astype(f32)
    own_standard = (own - center) * scale
    scaled = low.astype(f32).T * norm_gain[None, :]
    first_sum, second_sum = row_sums[0][:, None] / feats, row_sums[1][:, None] / feats
    stream_grad = ((scaled - first_sum - own_standard * second_sum) * scale).astype(bf16)
    return (
        stream_grad.reshape(own_slots, window, wf),
        weight[:, :wd],
        factor * vector[:wd],
        weight[:, wd:],
        factor * vector[wd:wt],
        gain_grad,
    )


def solution(mesh):
    parts = Mesh(
        mesh.devices.reshape(tuple(EXTENT[axis] for axis in ("g", "y", "x", "c", "m"))),
        ("g", "y", "x", "c", "m"),
    )
    every = ("g",) + DP
    placed = (
        P("g", DP, "m"),
        P("g", DP, "m"),
        P(DP, "m"),
        P("g", DP, "m"),
        P("g", DP, "m"),
        P(DP, "m"),
        P("g", None),
        P(every),
        P(every, None, "m"),
        P("m"),
        P(None, "m"),
        P("m"),
        P(None, "m"),
        P("m"),
    )
    return jax.shard_map(
        local,
        mesh=parts,
        in_specs=placed,
        out_specs=(
            P(every, None, "m"),
            P(every, "m"),
            P("m"),
            P(every, "m"),
            P("m"),
            P("m"),
        ),
        check_vma=False,
    )
```

```python
import jax
import jax.numpy as jnp
from jax import lax
from jax.sharding import Mesh
from jax.sharding import PartitionSpec as P

eps = 1e-06
loss_weight = 1024.0
f32 = jnp.float32
bf16 = jnp.bfloat16

EXTENT = {"g": 4, "y": 4, "x": 4, "c": 2, "m": 4}
DP = ("y", "x", "c")


def swap(array):
    return lax.ppermute(array, "c", [(0, 1), (1, 0)])


def exchange(array, axis):
    return lax.all_to_all(array, axis, split_axis=0, concat_axis=0, tiled=True)


def dot(a, b):
    return jnp.dot(a, b, preferred_element_type=f32)


def dot_last(a, b):
    return lax.dot_general(a, b, (((1,), (1,)), ((), ())), preferred_element_type=f32)


def dot_rows(a, b):
    return lax.dot_general(a, b, (((0,), (0,)), ((), ())), preferred_element_type=f32)


def one_hot(picked, width):
    return (lax.broadcasted_iota(jnp.int32, (picked.shape[0], width), 1) == picked[:, None]).astype(
        bf16
    )


def split(array, count):
    terms = []
    for _ in range(count):
        term = lax.reduce_precision(array, 8, 7)
        terms.append(term.astype(bf16))
        array = array - term
    return terms


def to_rows(vector, width):
    terms = jnp.concatenate(split(vector, 2))
    rows = -(-terms.shape[0] // (8 * width)) * 8
    return jnp.pad(terms, (0, rows * width - terms.shape[0])).reshape(rows, width)


def from_rows(rows, length):
    terms = rows.astype(f32).reshape(*rows.shape[:-2], -1)
    return terms[..., :length] + terms[..., length : 2 * length]


def head_grad(out, target, inner, square, tsquare, live):
    inverse = lax.rsqrt(square + eps) * lax.rsqrt(tsquare + eps)
    cosine = inner * inverse
    return -loss_weight * live * (target * inverse - cosine * out / (square + eps))


def local(
    dino_context,
    dino_stream,
    dino_out_proj,
    sam_context,
    sam_stream,
    sam_out_proj,
    owners,
    valid_rows,
    student_stream,
    norm_gain,
    adapt_dino,
    adapt_dino_bias,
    adapt_sam,
    adapt_sam_bias,
):
    m, c = lax.axis_index("m"), lax.axis_index("c")
    slots, per_peer, wd = dino_context.shape
    ws = sam_context.shape[2]
    rows = slots * per_peer
    own_slots, window, wf = student_stream.shape
    wt = wd + ws
    feats = wf * EXTENT["m"]
    peers = slots // own_slots
    kd, ks = dino_out_proj.shape[0], sam_out_proj.shape[0]

    context = jnp.concatenate(
        [dino_context.reshape(rows, wd), sam_context.reshape(rows, ws)], axis=1
    )
    context, student_stream, dino_out_proj, sam_out_proj, norm_gain = lax.optimization_barrier(
        (context, student_stream, dino_out_proj, sam_out_proj, norm_gain)
    )
    context = lax.all_gather(context, "m", axis=0, tiled=False)
    gain_terms = jnp.pad(jnp.stack(split(norm_gain, 3)), ((0, 5), (0, 0)))
    student = jnp.concatenate([student_stream.reshape(rows, wf), gain_terms], axis=0)
    student = lax.all_gather(student, "m", axis=1, tiled=True)
    packed = jnp.concatenate(
        [dino_out_proj, jnp.pad(sam_out_proj, ((0, 0), (0, wd - ws)))], axis=0
    )
    proj = exchange(jnp.tile(packed, (peers, 1)), DP).reshape(peers, kd + ks, wd)
    dino_proj = proj[:, :kd].reshape(4, wd, wd)
    sam_proj = proj[:, kd:, :ws].reshape(4, ws, ws)

    dino_mixed = sum(dot(context[j, :, :wd], dino_proj[j]) for j in range(4))
    sam_mixed = sum(dot(context[j, :, wd:], sam_proj[j]) for j in range(4))
    dino_feat = (dino_stream.reshape(rows, wd).astype(f32) + dino_mixed).astype(bf16)
    sam_feat = (sam_stream.reshape(rows, ws).astype(f32) + sam_mixed).astype(bf16)
    feat = jnp.concatenate([dino_feat, sam_feat], axis=1)
    image_row = jnp.arange(per_peer, dtype=jnp.int32)[None, :]
    goes_to = (owners[0][:, None] * per_peer + image_row).reshape(-1)
    sent = dot_rows(one_hot(goes_to, rows), feat).astype(bf16)
    arrived = exchange(sent, DP)
    place = jnp.arange(rows, dtype=jnp.int32)
    slot, row = place // window, place % window
    source = (row // per_peer) * (own_slots * per_peer) + slot * per_peer + row % per_peer
    target = dot(one_hot(source, rows), arrived)
    dino_target, sam_target = target[:, :wd], target[:, wd:]

    live = (
        (jnp.arange(window, dtype=jnp.int32)[None, :] < valid_rows[:, None])
        .astype(f32)
        .reshape(rows, 1)
    )
    values = student[:rows].astype(f32)
    gain = jnp.sum(student[rows:].astype(f32), axis=0, keepdims=True)
    center = jnp.sum(values, axis=1, keepdims=True) / feats
    spread = jnp.sum(values * values, axis=1, keepdims=True) / feats - center * center
    scale = lax.rsqrt(spread + eps)
    standard = (values - center) * scale
    normed = (standard * gain).astype(bf16)
    adapt = jnp.concatenate([adapt_dino, adapt_sam], axis=1)
    out = dot(normed, adapt) + jnp.concatenate([adapt_dino_bias, adapt_sam_bias])[None, :]
    dino_out, sam_out = out[:, :wd], out[:, wd:]
    each = feats // (EXTENT["g"] * peers)
    spot = jnp.arange(feats, dtype=jnp.int32)
    i, rest = spot % each, spot // each
    g_of, rest = rest % 4, rest // 4
    x_of, rest = rest % 4, rest // 4
    y_of, c_of = rest % 4, (rest // 4 + c) % 2
    feature = (((g_of * 4 + y_of) * 4 + x_of) * 2 + c_of) * each + i
    dealt = dot_last(normed, one_hot(feature, feats)).astype(bf16)

    stats = lax.psum(
        jnp.stack(
            [
                jnp.sum(dino_out * dino_target, axis=1),
                jnp.sum(dino_out * dino_out, axis=1),
                jnp.sum(dino_target * dino_target, axis=1),
                jnp.sum(sam_out * sam_target, axis=1),
                jnp.sum(sam_out * sam_out, axis=1),
                jnp.sum(sam_target * sam_target, axis=1),
            ]
        ),
        "m",
    )[:, :, None]
    dino_grad = head_grad(dino_out, dino_target, stats[0], stats[1], stats[2], live)
    sam_grad = head_grad(sam_out, sam_target, stats[3], stats[4], stats[5], live)
    grad = jnp.concatenate([dino_grad, sam_grad], axis=1)
    back = grad.astype(bf16)

    partial = dot_last(adapt, back)
    low = lax.psum_scatter(partial.astype(bf16), "m", scatter_dimension=0, tiled=True)
    scaled_part = partial * gain.T
    row_sums = jnp.stack(
        [jnp.sum(scaled_part, axis=0), jnp.sum(scaled_part * standard.T, axis=0)]
    )
    gain_part = jnp.sum(partial * standard.T, axis=1)

    half = feats // 2
    length = wt + feats + 1
    vector = jnp.concatenate([jnp.sum(grad, axis=0), gain_part, jnp.sum(live).reshape(1)])
    mine = dot_rows(dealt[:, :half], back)
    theirs = dot_rows(dealt[:, half:], back).astype(bf16)
    received = swap(jnp.concatenate([theirs, to_rows(vector, wt)], axis=0))
    chip = (mine + received[:half].astype(f32)).astype(bf16)
    vector = vector + from_rows(received[half:], length)
    beside = to_rows(vector, wt)
    chip = jnp.concatenate(
        [chip.reshape(16, -1, wt), jnp.broadcast_to(beside[None], (16,) + beside.shape)], axis=1
    )
    slab = exchange(chip.reshape(-1, wt), ("y", "x")).reshape(chip.shape)
    scaled = low.astype(f32).T * norm_gain[None, :]
    slab, scaled = lax.optimization_barrier((slab, scaled))
    strip = 4 * each
    weight = jnp.sum(slab[:, :strip].astype(f32), axis=0).astype(bf16)
    vector = jnp.sum(from_rows(slab[:, strip:], length), axis=0)
    beside = to_rows(vector, wt)
    deal = jnp.concatenate(
        [weight.reshape(4, each, wt), jnp.broadcast_to(beside[None], (4,) + beside.shape)], axis=1
    )
    share = exchange(deal.reshape(-1, wt), "g").reshape(deal.shape)
    weight = jnp.sum(share[:, :each].astype(f32), axis=0)
    vector = jnp.sum(from_rows(share[:, each:], length), axis=0)
    factor = lax.rsqrt(vector[-1])
    weight = (factor * weight).astype(bf16)
    sums = lax.psum(jnp.concatenate([row_sums.reshape(-1), vector[wt:-1]]), "m")
    row_sums = sums[: 2 * rows].reshape(2, rows)
    gain_grad = factor * lax.dynamic_slice_in_dim(sums, 2 * rows + m * wf, wf)

    own = student_stream.reshape(rows, wf).astype(f32)
    own_standard = (own - center) * scale
    first_sum, second_sum = row_sums[0][:, None] / feats, row_sums[1][:, None] / feats
    stream_grad = ((scaled - first_sum - own_standard * second_sum) * scale).astype(bf16)
    return (
        stream_grad.reshape(own_slots, window, wf),
        weight[:, :wd],
        factor * vector[:wd],
        weight[:, wd:],
        factor * vector[wd:wt],
        gain_grad,
    )


def solution(mesh):
    parts = Mesh(
        mesh.devices.reshape(tuple(EXTENT[axis] for axis in ("g", "y", "x", "c", "m"))),
        ("g", "y", "x", "c", "m"),
    )
    every = ("g",) + DP
    placed = (
        P("g", DP, "m"),
        P("g", DP, "m"),
        P(DP, "m"),
        P("g", DP, "m"),
        P("g", DP, "m"),
        P(DP, "m"),
        P("g", None),
        P(every),
        P(every, None, "m"),
        P("m"),
        P(None, "m"),
        P("m"),
        P(None, "m"),
        P("m"),
    )
    return jax.shard_map(
        local,
        mesh=parts,
        in_specs=placed,
        out_specs=(
            P(every, None, "m"),
            P(every, "m"),
            P("m"),
            P(every, "m"),
            P("m"),
            P("m"),
        ),
        check_vma=False,
    )
```

```python
import jax
import jax.numpy as jnp
from jax import lax
from jax.sharding import Mesh
from jax.sharding import PartitionSpec as P

eps = 1e-06
loss_weight = 1024.0
f32 = jnp.float32
bf16 = jnp.bfloat16

EXTENT = {"g": 4, "y": 4, "x": 4, "c": 2, "m": 4}
DP = ("y", "x", "c")


def shift_m(array, by):
    return lax.ppermute(array, "m", [(i, (i + by) % 4) for i in range(4)])


def exchange(array, axis):
    return lax.all_to_all(array, axis, split_axis=0, concat_axis=0, tiled=True)


def dot(a, b):
    return jnp.dot(a, b, preferred_element_type=f32)


def dot_last(a, b):
    return lax.dot_general(a, b, (((1,), (1,)), ((), ())), preferred_element_type=f32)


def dot_rows(a, b):
    return lax.dot_general(a, b, (((0,), (0,)), ((), ())), preferred_element_type=f32)


def one_hot(picked, width):
    return (lax.broadcasted_iota(jnp.int32, (picked.shape[0], width), 1) == picked[:, None]).astype(
        bf16
    )


def split(array, count):
    terms = []
    for _ in range(count):
        term = lax.reduce_precision(array, 8, 7)
        terms.append(term.astype(bf16))
        array = array - term
    return terms


def to_rows(vector, width):
    terms = jnp.concatenate(split(vector, 2))
    rows = -(-terms.shape[0] // (8 * width)) * 8
    return jnp.pad(terms, (0, rows * width - terms.shape[0])).reshape(rows, width)


def from_rows(rows, length):
    terms = rows.astype(f32).reshape(*rows.shape[:-2], -1)
    return terms[..., :length] + terms[..., length : 2 * length]


def head_grad(out, target, inner, square, tsquare, live):
    inverse = lax.rsqrt(square + eps) * lax.rsqrt(tsquare + eps)
    cosine = inner * inverse
    return -loss_weight * live * (target * inverse - cosine * out / (square + eps))


def local(
    dino_context,
    dino_stream,
    dino_out_proj,
    sam_context,
    sam_stream,
    sam_out_proj,
    owners,
    valid_rows,
    student_stream,
    norm_gain,
    adapt_dino,
    adapt_dino_bias,
    adapt_sam,
    adapt_sam_bias,
):
    m = lax.axis_index("m")
    slots, per_peer, wd = dino_context.shape
    ws = sam_context.shape[2]
    rows = slots * per_peer
    own_slots, window, wf = student_stream.shape
    wt = wd + ws
    feats = wf * EXTENT["m"]
    peers = slots // own_slots
    kd, ks = dino_out_proj.shape[0], sam_out_proj.shape[0]

    dino_full = lax.all_gather(dino_context.reshape(rows, wd), "m", axis=1, tiled=True)
    sam_full = lax.all_gather(sam_context.reshape(rows, ws), "m", axis=1, tiled=True)
    packed = jnp.concatenate(
        [dino_out_proj, jnp.pad(sam_out_proj, ((0, 0), (0, wd - ws)))], axis=0
    )
    proj = exchange(jnp.tile(packed, (peers, 1)), DP).reshape(peers, kd + ks, wd)
    dino_proj = proj[:, :kd].reshape(peers * kd, wd)
    sam_proj = proj[:, kd:, :ws].reshape(peers * ks, ws)

    dino_mixed = dot(dino_full, dino_proj)
    sam_mixed = dot(sam_full, sam_proj)
    dino_feat = (dino_stream.reshape(rows, wd).astype(f32) + dino_mixed).astype(bf16)
    sam_feat = (sam_stream.reshape(rows, ws).astype(f32) + sam_mixed).astype(bf16)
    feat = jnp.concatenate([dino_feat, sam_feat], axis=1)
    image_row = jnp.arange(per_peer, dtype=jnp.int32)[None, :]
    goes_to = (owners[0][:, None] * per_peer + image_row).reshape(-1)
    sent = dot_rows(one_hot(goes_to, rows), feat).astype(bf16)
    gain_terms = jnp.pad(jnp.stack(split(norm_gain, 3)), ((0, 5), (0, 0)))
    student = jnp.concatenate([student_stream.reshape(rows, wf), gain_terms], axis=0)
    sent, student = lax.optimization_barrier((sent, student))
    arrived = exchange(sent, DP)
    student = lax.all_gather(student, "m", axis=1, tiled=True)
    arrived, student = lax.optimization_barrier((arrived, student))
    place = jnp.arange(rows, dtype=jnp.int32)
    slot, row = place // window, place % window
    source = (row // per_peer) * (own_slots * per_peer) + slot * per_peer + row % per_peer
    target = dot(one_hot(source, rows), arrived)
    dino_target, sam_target = target[:, :wd], target[:, wd:]

    live = (
        (jnp.arange(window, dtype=jnp.int32)[None, :] < valid_rows[:, None])
        .astype(f32)
        .reshape(rows, 1)
    )
    values = student[:rows].astype(f32)
    gain = jnp.sum(student[rows:].astype(f32), axis=0, keepdims=True)
    center = jnp.sum(values, axis=1, keepdims=True) / feats
    spread = jnp.sum(values * values, axis=1, keepdims=True) / feats - center * center
    scale = lax.rsqrt(spread + eps)
    standard = (values - center) * scale
    normed = (standard * gain).astype(bf16)
    adapt = jnp.concatenate([adapt_dino, adapt_sam], axis=1)
    out = dot(normed, adapt) + jnp.concatenate([adapt_dino_bias, adapt_sam_bias])[None, :]
    dino_out, sam_out = out[:, :wd], out[:, wd:]
    each = feats // (EXTENT["g"] * peers)
    strip = EXTENT["g"] * each
    block = strip + 8
    spot = jnp.arange(peers * block, dtype=jnp.int32)
    inside = spot % block
    feature = (inside // each * peers + spot // block) * each + inside % each
    dealt = dot_last(one_hot(jnp.where(inside < strip, feature, -1), feats), normed).astype(bf16)
    dealt = jnp.concatenate([dealt, one_hot(jnp.where(inside < strip, -1, inside - strip), 16)], axis=1)

    stats = lax.psum(
        jnp.stack(
            [
                jnp.sum(dino_out * dino_target, axis=1),
                jnp.sum(dino_out * dino_out, axis=1),
                jnp.sum(dino_target * dino_target, axis=1),
                jnp.sum(sam_out * sam_target, axis=1),
                jnp.sum(sam_out * sam_out, axis=1),
                jnp.sum(sam_target * sam_target, axis=1),
            ]
        ),
        "m",
    )[:, :, None]
    dino_grad = head_grad(dino_out, dino_target, stats[0], stats[1], stats[2], live)
    sam_grad = head_grad(sam_out, sam_target, stats[3], stats[4], stats[5], live)
    grad = jnp.concatenate([dino_grad, sam_grad], axis=1)
    back = grad.astype(bf16)

    partial = dot_last(adapt, back)
    scaled_part = partial * gain.T
    row_sums = jnp.stack(
        [jnp.sum(scaled_part, axis=0), jnp.sum(scaled_part * standard.T, axis=0)]
    )
    gain_part = jnp.sum(partial * standard.T, axis=1)

    length = wt + feats + 1
    vector = jnp.concatenate([jnp.sum(grad, axis=0), gain_part, jnp.sum(live).reshape(1)])
    beside = to_rows(vector, wt)
    under = jnp.concatenate([back, jnp.pad(beside, ((0, 16 - beside.shape[0]), (0, 0)))], axis=0)
    weight = dot(dealt, under).astype(bf16)
    parts = partial.astype(bf16).reshape(4, wf, rows)
    slab = exchange(weight, DP).reshape(peers, block, wt)
    normed_grad = sum(
        part.astype(f32)
        for part in [lax.dynamic_index_in_dim(parts, m, 0, False)]
        + [
            shift_m(lax.dynamic_index_in_dim(parts, (m + by) % 4, 0, False), by)
            for by in (2, 1, 3)
        ]
    )
    weight = jnp.sum(slab[:, :strip].astype(f32), axis=0).astype(bf16)
    vector = jnp.sum(from_rows(slab[:, strip:], length), axis=0)
    beside = to_rows(vector, wt)
    deal = jnp.concatenate(
        [weight.reshape(4, each, wt), jnp.broadcast_to(beside[None], (4,) + beside.shape)], axis=1
    )
    deal, normed_grad = lax.optimization_barrier((deal, normed_grad))
    share = exchange(deal.reshape(-1, wt), "g").reshape(deal.shape)
    weight = jnp.sum(share[:, :each].astype(f32), axis=0)
    vector = jnp.sum(from_rows(share[:, each:], length), axis=0)
    factor = lax.rsqrt(vector[-1])
    weight = (factor * weight).astype(bf16)
    sums = lax.psum(jnp.concatenate([row_sums.reshape(-1), vector[wt:-1]]), "m")
    row_sums = sums[: 2 * rows].reshape(2, rows)
    gain_grad = factor * lax.dynamic_slice_in_dim(sums, 2 * rows + m * wf, wf)

    own = student_stream.reshape(rows, wf).astype(f32)
    own_standard = (own - center) * scale
    scaled = normed_grad.T * norm_gain[None, :]
    first_sum, second_sum = row_sums[0][:, None] / feats, row_sums[1][:, None] / feats
    stream_grad = ((scaled - first_sum - own_standard * second_sum) * scale).astype(bf16)
    return (
        stream_grad.reshape(own_slots, window, wf),
        weight[:, :wd],
        factor * vector[:wd],
        weight[:, wd:],
        factor * vector[wd:wt],
        gain_grad,
    )


def solution(mesh):
    parts = Mesh(
        mesh.devices.reshape(tuple(EXTENT[axis] for axis in ("g", "y", "x", "c", "m"))),
        ("g", "y", "x", "c", "m"),
    )
    every = ("g",) + DP
    placed = (
        P("g", DP, "m"),
        P("g", DP, "m"),
        P(DP, "m"),
        P("g", DP, "m"),
        P("g", DP, "m"),
        P(DP, "m"),
        P("g", None),
        P(every),
        P(every, None, "m"),
        P("m"),
        P(None, "m"),
        P("m"),
        P(None, "m"),
        P("m"),
    )
    return jax.shard_map(
        local,
        mesh=parts,
        in_specs=placed,
        out_specs=(
            P(every, None, "m"),
            P(every, "m"),
            P("m"),
            P(every, "m"),
            P("m"),
            P("m"),
        ),
        check_vma=False,
    )
```

```python
import jax
import jax.numpy as jnp
from jax import lax
from jax.experimental import pallas as pl
from jax.experimental.pallas import tpu as pltpu
from jax.sharding import Mesh
from jax.sharding import PartitionSpec as P

eps = 1e-06
loss_weight = 1024.0
f32 = jnp.float32
bf16 = jnp.bfloat16

EXTENT = {"g": 4, "y": 4, "x": 4, "c": 2, "m": 4}
DP = ("y", "x", "c")


def shift_m(array, by):
    return lax.ppermute(array, "m", [(i, (i + by) % 4) for i in range(4)])


def exchange(array, axis):
    return lax.all_to_all(array, axis, split_axis=0, concat_axis=0, tiled=True)


def dot(a, b):
    return jnp.dot(a, b, preferred_element_type=f32)


def dot_last(a, b):
    return lax.dot_general(a, b, (((1,), (1,)), ((), ())), preferred_element_type=f32)


def dot_rows(a, b):
    return lax.dot_general(a, b, (((0,), (0,)), ((), ())), preferred_element_type=f32)


def one_hot(picked, width):
    return (lax.broadcasted_iota(jnp.int32, (picked.shape[0], width), 1) == picked[:, None]).astype(
        bf16
    )


def split(array, count):
    terms = []
    for _ in range(count):
        term = lax.reduce_precision(array, 8, 7)
        terms.append(term.astype(bf16))
        array = array - term
    return terms


def split_rows(rows):
    term = lax.reduce_precision(rows, 8, 7)
    return jnp.concatenate([term, lax.reduce_precision(rows - term, 8, 7)], axis=0)


def summed_rows(pieces):
    rows = jnp.sum(pieces.astype(f32), axis=0)
    return rows[:4] + rows[4:]


def payload_kernel(dealt_ref, back_ref, beside_ref, out_ref):
    block = beside_ref.shape[0]
    step = 8 * block
    for start in range(0, dealt_ref.shape[0], step):
        rows = pl.ds(start, step)
        weight = dot(dealt_ref[rows, :], back_ref[...])
        whole = weight.reshape(8, block, weight.shape[1]) + beside_ref[...][None]
        out_ref[rows, :] = whole.reshape(weight.shape).astype(bf16)


def payload(dealt, back, beside):
    n, k = dealt.shape
    wt = back.shape[1]
    return pl.pallas_call(
        payload_kernel,
        out_shape=jax.ShapeDtypeStruct((n, wt), bf16),
        in_specs=[pl.BlockSpec(memory_space=pltpu.VMEM)] * 3,
        out_specs=pl.BlockSpec(memory_space=pltpu.VMEM),
        compiler_params=pltpu.CompilerParams(vmem_limit_bytes=24 * 2**20),
        cost_estimate=pl.CostEstimate(
            flops=2 * n * k * wt, bytes_accessed=2 * (n * k + k * wt + n * wt), transcendentals=0
        ),
    )(dealt, back, beside)


def head_grad(out, target, inner, square, tsquare, live):
    inverse = lax.rsqrt(square + eps) * lax.rsqrt(tsquare + eps)
    cosine = inner * inverse
    return -loss_weight * live * (target * inverse - cosine * out / (square + eps))


def local(
    dino_context,
    dino_stream,
    dino_out_proj,
    sam_context,
    sam_stream,
    sam_out_proj,
    owners,
    valid_rows,
    student_stream,
    norm_gain,
    adapt_dino,
    adapt_dino_bias,
    adapt_sam,
    adapt_sam_bias,
):
    m = lax.axis_index("m")
    slots, per_peer, wd = dino_context.shape
    ws = sam_context.shape[2]
    rows = slots * per_peer
    own_slots, window, wf = student_stream.shape
    wt = wd + ws
    feats = wf * EXTENT["m"]
    peers = slots // own_slots
    kd, ks = dino_out_proj.shape[0], sam_out_proj.shape[0]

    dino_full = lax.all_gather(dino_context.reshape(rows, wd), "m", axis=1, tiled=True)
    sam_full = lax.all_gather(sam_context.reshape(rows, ws), "m", axis=1, tiled=True)
    packed = jnp.concatenate(
        [dino_out_proj, jnp.pad(sam_out_proj, ((0, 0), (0, wd - ws)))], axis=0
    )
    proj = exchange(jnp.tile(packed, (peers, 1)), DP).reshape(peers, kd + ks, wd)
    dino_proj = proj[:, :kd].reshape(peers * kd, wd)
    sam_proj = proj[:, kd:, :ws].reshape(peers * ks, ws)

    dino_mixed = dot(dino_full, dino_proj)
    sam_mixed = dot(sam_full, sam_proj)
    dino_feat = (dino_stream.reshape(rows, wd).astype(f32) + dino_mixed).astype(bf16)
    sam_feat = (sam_stream.reshape(rows, ws).astype(f32) + sam_mixed).astype(bf16)
    feat = jnp.concatenate([dino_feat, sam_feat], axis=1)
    image_row = jnp.arange(per_peer, dtype=jnp.int32)[None, :]
    goes_to = (owners[0][:, None] * per_peer + image_row).reshape(-1)
    sent = dot_rows(one_hot(goes_to, rows), feat).astype(bf16)
    gain_terms = jnp.pad(jnp.stack(split(norm_gain, 3)), ((0, 5), (0, 0)))
    student = jnp.concatenate([student_stream.reshape(rows, wf), gain_terms], axis=0)
    sent, student = lax.optimization_barrier((sent, student))
    arrived = exchange(sent, DP)
    student = lax.all_gather(student, "m", axis=1, tiled=True)
    arrived, student = lax.optimization_barrier((arrived, student))
    place = jnp.arange(rows, dtype=jnp.int32)
    slot, row = place // window, place % window
    source = (row // per_peer) * (own_slots * per_peer) + slot * per_peer + row % per_peer
    target = dot(one_hot(source, rows), arrived)
    dino_target, sam_target = target[:, :wd], target[:, wd:]

    live = (
        (jnp.arange(window, dtype=jnp.int32)[None, :] < valid_rows[:, None])
        .astype(f32)
        .reshape(rows, 1)
    )
    values = student[:rows].astype(f32)
    gain = jnp.sum(student[rows:].astype(f32), axis=0, keepdims=True)
    center = jnp.sum(values, axis=1, keepdims=True) / feats
    spread = jnp.sum(values * values, axis=1, keepdims=True) / feats - center * center
    scale = lax.rsqrt(spread + eps)
    standard = (values - center) * scale
    normed = (standard * gain).astype(bf16)
    adapt = jnp.concatenate([adapt_dino, adapt_sam], axis=1)
    out = dot(normed, adapt) + jnp.concatenate([adapt_dino_bias, adapt_sam_bias])[None, :]
    dino_out, sam_out = out[:, :wd], out[:, wd:]
    each = feats // (EXTENT["g"] * peers)
    strip = EXTENT["g"] * each
    block = strip + 8
    spot = jnp.arange(peers * block, dtype=jnp.int32)
    inside = spot % block
    feature = (inside // each * peers + spot // block) * each + inside % each
    dealt = dot_last(one_hot(jnp.where(inside < strip, feature, -1), feats), normed).astype(bf16)

    stats = lax.psum(
        jnp.stack(
            [
                jnp.sum(dino_out * dino_target, axis=1),
                jnp.sum(dino_out * dino_out, axis=1),
                jnp.sum(dino_target * dino_target, axis=1),
                jnp.sum(sam_out * sam_target, axis=1),
                jnp.sum(sam_out * sam_out, axis=1),
                jnp.sum(sam_target * sam_target, axis=1),
            ]
        ),
        "m",
    )[:, :, None]
    dino_grad = head_grad(dino_out, dino_target, stats[0], stats[1], stats[2], live)
    sam_grad = head_grad(sam_out, sam_target, stats[3], stats[4], stats[5], live)
    grad = jnp.concatenate([dino_grad, sam_grad], axis=1)
    back = grad.astype(bf16)

    partial = dot_last(adapt, back)
    scaled_part = partial * gain.T
    row_sums = jnp.stack(
        [jnp.sum(scaled_part, axis=0), jnp.sum(scaled_part * standard.T, axis=0)]
    )
    gain_part = jnp.sum(partial * standard.T, axis=1)

    rest = feats - wt
    vector = jnp.stack(
        [
            jnp.sum(grad, axis=0),
            gain_part[:wt],
            jnp.pad(gain_part[wt:], (0, wt - rest)),
            jnp.full((wt,), jnp.sum(live)),
        ]
    )
    weight = payload(dealt, back, jnp.pad(split_rows(vector), ((strip, 0), (0, 0))))
    parts = partial.astype(bf16).reshape(4, wf, rows)
    slab = exchange(weight, DP).reshape(peers, block, wt)
    normed_grad = sum(
        part.astype(f32)
        for part in [lax.dynamic_index_in_dim(parts, m, 0, False)]
        + [
            shift_m(lax.dynamic_index_in_dim(parts, (m + by) % 4, 0, False), by)
            for by in (2, 1, 3)
        ]
    )
    weight = jnp.sum(slab[:, :strip].astype(f32), axis=0).astype(bf16)
    beside = split_rows(summed_rows(slab[:, strip:])).astype(bf16)
    deal = jnp.concatenate(
        [weight.reshape(4, each, wt), jnp.broadcast_to(beside[None], (4,) + beside.shape)], axis=1
    )
    deal, normed_grad = lax.optimization_barrier((deal, normed_grad))
    share = exchange(deal.reshape(-1, wt), "g").reshape(deal.shape)
    weight = jnp.sum(share[:, :each].astype(f32), axis=0)
    vector = summed_rows(share[:, each:])
    row_sums, gain_rows = lax.psum((row_sums, vector[1:3]), "m")
    factor = lax.rsqrt(vector[3, 0])
    weight = (factor * weight).astype(bf16)
    bias_grad = factor * vector[0]
    gain_grad = jnp.concatenate([gain_rows[0], gain_rows[1, :rest]])
    gain_grad = factor * lax.dynamic_slice_in_dim(gain_grad, m * wf, wf)

    own = student_stream.reshape(rows, wf).astype(f32)
    own_standard = (own - center) * scale
    scaled = normed_grad.T * norm_gain[None, :]
    first_sum, second_sum = row_sums[0][:, None] / feats, row_sums[1][:, None] / feats
    stream_grad = ((scaled - first_sum - own_standard * second_sum) * scale).astype(bf16)
    return (
        stream_grad.reshape(own_slots, window, wf),
        weight[:, :wd],
        bias_grad[:wd],
        weight[:, wd:],
        bias_grad[wd:],
        gain_grad,
    )


def solution(mesh):
    parts = Mesh(
        mesh.devices.reshape(tuple(EXTENT[axis] for axis in ("g", "y", "x", "c", "m"))),
        ("g", "y", "x", "c", "m"),
    )
    every = ("g",) + DP
    placed = (
        P("g", DP, "m"),
        P("g", DP, "m"),
        P(DP, "m"),
        P("g", DP, "m"),
        P("g", DP, "m"),
        P(DP, "m"),
        P("g", None),
        P(every),
        P(every, None, "m"),
        P("m"),
        P(None, "m"),
        P("m"),
        P(None, "m"),
        P("m"),
    )
    return jax.shard_map(
        local,
        mesh=parts,
        in_specs=placed,
        out_specs=(
            P(every, None, "m"),
            P(every, "m"),
            P("m"),
            P(every, "m"),
            P("m"),
            P("m"),
        ),
        check_vma=False,
    )
```

```python
import jax
import jax.numpy as jnp
from jax import lax
from jax.experimental import pallas as pl
from jax.experimental.pallas import tpu as pltpu
from jax.sharding import Mesh
from jax.sharding import PartitionSpec as P

eps = 1e-06
loss_weight = 1024.0
f32 = jnp.float32
bf16 = jnp.bfloat16

EXTENT = {"g": 4, "y": 4, "x": 4, "c": 2, "m": 4}
DP = ("y", "x", "c")


def shift_m(array, by):
    return lax.ppermute(array, "m", [(i, (i + by) % 4) for i in range(4)])


def exchange(array, axis):
    return lax.all_to_all(array, axis, split_axis=0, concat_axis=0, tiled=True)


def dot(a, b):
    return jnp.dot(a, b, preferred_element_type=f32)


def dot_last(a, b):
    return lax.dot_general(a, b, (((1,), (1,)), ((), ())), preferred_element_type=f32)


def dot_rows(a, b):
    return lax.dot_general(a, b, (((0,), (0,)), ((), ())), preferred_element_type=f32)


def one_hot(picked, width):
    return (lax.broadcasted_iota(jnp.int32, (picked.shape[0], width), 1) == picked[:, None]).astype(
        bf16
    )


def split(array, count):
    terms = []
    for _ in range(count):
        term = lax.reduce_precision(array, 8, 7)
        terms.append(term.astype(bf16))
        array = array - term
    return terms


def split_rows(rows):
    term = lax.reduce_precision(rows, 8, 7)
    return jnp.concatenate([term, lax.reduce_precision(rows - term, 8, 7)], axis=0)


def summed_rows(pieces):
    rows = jnp.sum(pieces.astype(f32), axis=0)
    return rows[:4] + rows[4:]


def payload_kernel(dealt_ref, back_ref, beside_ref, out_ref):
    block = beside_ref.shape[0]
    step = 8 * block
    for start in range(0, dealt_ref.shape[0], step):
        rows = pl.ds(start, step)
        weight = dot(dealt_ref[rows, :], back_ref[...])
        whole = weight.reshape(8, block, weight.shape[1]) + beside_ref[...][None]
        out_ref[rows, :] = whole.reshape(weight.shape).astype(bf16)


def payload(dealt, back, beside):
    n, k = dealt.shape
    wt = back.shape[1]
    return pl.pallas_call(
        payload_kernel,
        out_shape=jax.ShapeDtypeStruct((n, wt), bf16),
        in_specs=[pl.BlockSpec(memory_space=pltpu.VMEM)] * 3,
        out_specs=pl.BlockSpec(memory_space=pltpu.VMEM),
        compiler_params=pltpu.CompilerParams(vmem_limit_bytes=24 * 2**20),
        cost_estimate=pl.CostEstimate(
            flops=2 * n * k * wt, bytes_accessed=2 * (n * k + k * wt + n * wt), transcendentals=0
        ),
    )(dealt, back, beside)


def head_grad(out, target, inner, square, tsquare, live):
    inverse = lax.rsqrt(square + eps) * lax.rsqrt(tsquare + eps)
    cosine = inner * inverse
    return -loss_weight * live * (target * inverse - cosine * out / (square + eps))


def local(
    dino_context,
    dino_stream,
    dino_out_proj,
    sam_context,
    sam_stream,
    sam_out_proj,
    owners,
    valid_rows,
    student_stream,
    norm_gain,
    adapt_dino,
    adapt_dino_bias,
    adapt_sam,
    adapt_sam_bias,
):
    m = lax.axis_index("m")
    slots, per_peer, wd = dino_context.shape
    ws = sam_context.shape[2]
    rows = slots * per_peer
    own_slots, window, wf = student_stream.shape
    wt = wd + ws
    feats = wf * EXTENT["m"]
    peers = slots // own_slots
    kd, ks = dino_out_proj.shape[0], sam_out_proj.shape[0]

    dino_full = lax.all_gather(dino_context.reshape(rows, wd), "m", axis=1, tiled=True)
    sam_full = lax.all_gather(sam_context.reshape(rows, ws), "m", axis=1, tiled=True)
    packed = jnp.concatenate(
        [dino_out_proj, jnp.pad(sam_out_proj, ((0, 0), (0, wd - ws)))], axis=0
    )
    proj = exchange(jnp.tile(packed, (peers, 1)), DP).reshape(peers, kd + ks, wd)
    dino_proj = proj[:, :kd].reshape(peers * kd, wd)
    sam_proj = proj[:, kd:, :ws].reshape(peers * ks, ws)

    dino_mixed = dot(dino_full, dino_proj)
    sam_mixed = dot(sam_full, sam_proj)
    dino_feat = (dino_stream.reshape(rows, wd).astype(f32) + dino_mixed).astype(bf16)
    sam_feat = (sam_stream.reshape(rows, ws).astype(f32) + sam_mixed).astype(bf16)
    feat = jnp.concatenate([dino_feat, sam_feat], axis=1)
    image_row = jnp.arange(per_peer, dtype=jnp.int32)[None, :]
    goes_to = (owners[0][:, None] * per_peer + image_row).reshape(-1)
    sent = dot_rows(one_hot(goes_to, rows), feat).astype(bf16)
    spare = -3 * wf % rows
    gain_terms = jnp.pad(jnp.concatenate(split(norm_gain, 3)), (0, spare)).reshape(-1, rows)
    gain_terms = jnp.pad(gain_terms, ((0, -gain_terms.shape[0] % 8), (0, 0)))
    student = jnp.concatenate([student_stream.reshape(rows, wf).T, gain_terms], axis=0)
    sent, student = lax.optimization_barrier((sent, student))
    arrived = exchange(sent, DP)
    student = lax.all_gather(student, "m", axis=0, tiled=False)
    arrived, student = lax.optimization_barrier((arrived, student))
    place = jnp.arange(rows, dtype=jnp.int32)
    slot, row = place // window, place % window
    source = (row // per_peer) * (own_slots * per_peer) + slot * per_peer + row % per_peer
    target = dot(one_hot(source, rows), arrived)
    dino_target, sam_target = target[:, :wd], target[:, wd:]

    live = (
        (jnp.arange(window, dtype=jnp.int32)[None, :] < valid_rows[:, None])
        .astype(f32)
        .reshape(rows, 1)
    )
    values = student[:, :wf].reshape(feats, rows).T.astype(f32)
    gain = student[:, wf:].reshape(4, -1)[:, : 3 * wf].reshape(4, 3, wf).astype(f32)
    gain = jnp.sum(gain, axis=1).reshape(1, feats)
    center = jnp.sum(values, axis=1, keepdims=True) / feats
    spread = jnp.sum(values * values, axis=1, keepdims=True) / feats - center * center
    scale = lax.rsqrt(spread + eps)
    standard = (values - center) * scale
    normed = (standard * gain).astype(bf16)
    adapt = jnp.concatenate([adapt_dino, adapt_sam], axis=1)
    out = dot(normed, adapt) + jnp.concatenate([adapt_dino_bias, adapt_sam_bias])[None, :]
    dino_out, sam_out = out[:, :wd], out[:, wd:]
    each = feats // (EXTENT["g"] * peers)
    strip = EXTENT["g"] * each
    block = strip + 8
    spot = jnp.arange(peers * block, dtype=jnp.int32)
    inside = spot % block
    feature = (inside // each * peers + spot // block) * each + inside % each
    dealt = dot_last(one_hot(jnp.where(inside < strip, feature, -1), feats), normed).astype(bf16)

    stats = lax.psum(
        jnp.stack(
            [
                jnp.sum(dino_out * dino_target, axis=1),
                jnp.sum(dino_out * dino_out, axis=1),
                jnp.sum(dino_target * dino_target, axis=1),
                jnp.sum(sam_out * sam_target, axis=1),
                jnp.sum(sam_out * sam_out, axis=1),
                jnp.sum(sam_target * sam_target, axis=1),
            ]
        ),
        "m",
    )[:, :, None]
    dino_grad = head_grad(dino_out, dino_target, stats[0], stats[1], stats[2], live)
    sam_grad = head_grad(sam_out, sam_target, stats[3], stats[4], stats[5], live)
    grad = jnp.concatenate([dino_grad, sam_grad], axis=1)
    back = grad.astype(bf16)

    partial = dot_last(adapt, back)
    scaled_part = partial * gain.T
    row_sums = jnp.stack(
        [jnp.sum(scaled_part, axis=0), jnp.sum(scaled_part * standard.T, axis=0)]
    )
    gain_part = jnp.sum(partial * standard.T, axis=1)

    rest = feats - wt
    vector = jnp.stack(
        [
            jnp.sum(grad, axis=0),
            gain_part[:wt],
            jnp.pad(gain_part[wt:], (0, wt - rest)),
            jnp.full((wt,), jnp.sum(live)),
        ]
    )
    weight = payload(dealt, back, jnp.pad(split_rows(vector), ((strip, 0), (0, 0))))
    parts = partial.astype(bf16).reshape(4, wf, rows)
    slab = exchange(weight, DP).reshape(peers, block, wt)
    normed_grad = sum(
        part.astype(f32)
        for part in [lax.dynamic_index_in_dim(parts, m, 0, False)]
        + [
            shift_m(lax.dynamic_index_in_dim(parts, (m + by) % 4, 0, False), by)
            for by in (2, 1, 3)
        ]
    )
    weight = jnp.sum(slab[:, :strip].astype(f32), axis=0).astype(bf16)
    beside = split_rows(summed_rows(slab[:, strip:])).astype(bf16)
    deal = jnp.concatenate(
        [weight.reshape(4, each, wt), jnp.broadcast_to(beside[None], (4,) + beside.shape)], axis=1
    )
    deal, normed_grad = lax.optimization_barrier((deal, normed_grad))
    share = exchange(deal.reshape(-1, wt), "g").reshape(deal.shape)
    weight = jnp.sum(share[:, :each].astype(f32), axis=0)
    vector = summed_rows(share[:, each:])
    row_sums, gain_rows = lax.psum((row_sums, vector[1:3]), "m")
    factor = lax.rsqrt(vector[3, 0])
    weight = (factor * weight).astype(bf16)
    bias_grad = factor * vector[0]
    gain_grad = jnp.concatenate([gain_rows[0], gain_rows[1, :rest]])
    gain_grad = factor * lax.dynamic_slice_in_dim(gain_grad, m * wf, wf)

    own = student_stream.reshape(rows, wf).astype(f32)
    own_standard = (own - center) * scale
    scaled = normed_grad.T * norm_gain[None, :]
    first_sum, second_sum = row_sums[0][:, None] / feats, row_sums[1][:, None] / feats
    stream_grad = ((scaled - first_sum - own_standard * second_sum) * scale).astype(bf16)
    return (
        stream_grad.reshape(own_slots, window, wf),
        weight[:, :wd],
        bias_grad[:wd],
        weight[:, wd:],
        bias_grad[wd:],
        gain_grad,
    )


def solution(mesh):
    parts = Mesh(
        mesh.devices.reshape(tuple(EXTENT[axis] for axis in ("g", "y", "x", "c", "m"))),
        ("g", "y", "x", "c", "m"),
    )
    every = ("g",) + DP
    placed = (
        P("g", DP, "m"),
        P("g", DP, "m"),
        P(DP, "m"),
        P("g", DP, "m"),
        P("g", DP, "m"),
        P(DP, "m"),
        P("g", None),
        P(every),
        P(every, None, "m"),
        P("m"),
        P(None, "m"),
        P("m"),
        P(None, "m"),
        P("m"),
    )
    return jax.shard_map(
        local,
        mesh=parts,
        in_specs=placed,
        out_specs=(
            P(every, None, "m"),
            P(every, "m"),
            P("m"),
            P(every, "m"),
            P("m"),
            P("m"),
        ),
        check_vma=False,
    )
```
